256 devices in a mesh: fsdp: 64 (over y, x_hi, z), tensor: 4 (over x_lo, core).
Axes of the slice: x: 4 (x_hi: 2, x_lo: 2; x = x_hi * 2 + x_lo), y: 4, z: 8, core: 2. Of those that a mesh axis runs over, the one named last changes fastest.
Arguments:
- activations: bfloat16 [98304, 5120], P('fsdp', 'tensor'), may hold values from -6 to 6
- key_weight: bfloat16 [5120, 1024], P('tensor'), may hold values from -0.078125 to 0.078125
- key_gain: float32 [128], replicated, may hold values from 0.1 to 1.9
- span_start: int32 [64], P('fsdp'), may hold values from 0 to 4095
- next_weight: bfloat16 [2, 5120, 1024], P(None, ('fsdp', 'tensor')), may hold values from -16 to 16
Outputs:
- new_keys: bfloat16 [98304, 1024], P('fsdp', 'tensor')
- next_scaled: bfloat16 [2, 5120, 1024], P(None, None, 'tensor')
- block_max: float32 [2, 40, 8], P(None, None, 'tensor')
The draws below stay inside these ranges and needn't reach their ends.
All inputs are finite; a program needn't handle non-finite values. Where the reference program divides by a largest or mean magnitude, that divisor is 1e-20 or more.
Results may differ from the reference program's by a relative error of at most 0.015.
Values may be sent and summed in bfloat16 or wider, within the bound.
No kernel may reach another device: no remote copies, remote signals or barrier semaphores. Data moves between devices by JAX's collectives and lax.ppermute only.
A program may use at most 128 MiB of HBM per device.

```python
import math
import jax
import jax.numpy as jnp
from jax import lax

D = 5120
HD = 128
TOK = 1536
LAYERS = 2
BLOCK = 128
KD = 1024
TOKENS = 98304
N_FSDP = 64
N_TENSOR = 4


def draw_next_weight(key, part):
    key = jax.random.fold_in(key, 7)
    base_key, row_key, col_key = jax.random.split(key, 3)
    base = jnp.clip(jax.random.normal(base_key, (LAYERS, D, KD), jnp.float32), -4.0, 4.0)
    row_scale = jnp.exp(jax.random.uniform(row_key, (LAYERS, D, 1), jnp.float32, 0.0, math.log(10.0)))
    col_scale = jnp.exp(jax.random.uniform(col_key, (LAYERS, 1, KD), jnp.float32, 0.0, math.log(10.0)))
    weights = base * row_scale * col_scale / 25.0
    return weights.astype(jnp.bfloat16)


def place_ends(drawn, key, low, high):
    index_at = [jax.random.randint(jax.random.fold_in(key, axis), (), 0, length) for axis, length in enumerate(drawn.shape)]
    main_axis = drawn.shape.index(max(drawn.shape))
    next_to = index_at[:main_axis] + [(index_at[main_axis] + 1) % drawn.shape[main_axis]] + index_at[main_axis + 1:]
    return drawn.at[tuple(index_at)].set(low).at[tuple(next_to)].set(high)


def shard_levels(own_key, shape, cuts, least, top_value):
    def one(axis_at, parts):
        draws = jax.random.uniform(jax.random.fold_in(jax.random.fold_in(own_key, 6), axis_at), (parts,), jnp.float32, least / len(cuts), top_value / len(cuts))
        return jnp.repeat(jnp.exp(draws), shape[axis_at] // parts).reshape((-1,) + (1,) * (len(shape) - axis_at - 1))

    level = one(*cuts[0])
    for cut in cuts[1:]:
        level = level * one(*cut)
    return level


def gaussian(rng, dims, deviation, bound, cuts=(), kind=jnp.bfloat16):
    entries = jax.random.normal(rng, dims, jnp.float32) * deviation
    if len(cuts) > 0:
        entries = shard_levels(rng, dims, cuts, -0.22, 0.18) * entries
    return jnp.clip(entries, min=-bound, max=bound).astype(kind)


def setup_inputs(seed: int = 0) -> dict:
    splits = jax.random.split(jax.random.key(seed), 6)
    return {
        "activations": gaussian(splits[0], (TOKENS, D), 1.0, 6.0, ((0, 64), (1, 4))),
        "key_weight": gaussian(splits[1], (D, KD), D ** -0.5, 0.078125, ((0, 4),)),
        "key_gain": jnp.clip(1.0 + 0.18 * jax.random.normal(splits[2], (HD,), jnp.float32), 0.1, 1.9),
        "span_start": place_ends(jax.random.randint(splits[3], (N_FSDP,), 0, 4096), jax.random.fold_in(splits[3], 1), 0, 4095).astype(jnp.int32),
        "next_weight": draw_next_weight(jax.random.fold_in(splits[5], 71), 0),
    }


def finish_keys(running, span_begin, key_gain):
    token_count = running.shape[0]
    head_size = key_gain.shape[0]
    half_size = head_size // 2
    head_view = running.reshape(token_count, -1, head_size)
    normed = head_view * lax.rsqrt(lax.optimization_barrier(jnp.mean(head_view * head_view, axis=-1, keepdims=True)) + 1e-06) * key_gain
    positions = (span_begin + jnp.arange(token_count, dtype=jnp.int32)).astype(jnp.float32)
    frequency = jnp.exp(jnp.arange(half_size, dtype=jnp.float32) * (-2.0 * math.log(1000000.0) / head_size))
    angles = positions[:, None] * frequency[None, :]
    cosine = jnp.cos(angles)[:, None, :]
    sine_part = jnp.sin(angles)[:, None, :]
    lower_half = normed[..., :half_size]
    upper_half = normed[..., half_size:]
    rotated = jnp.concatenate([lower_half * cosine - upper_half * sine_part, upper_half * cosine + lower_half * sine_part], axis=-1)
    return rotated.reshape(token_count, -1).astype(jnp.bfloat16)

def quantize(weights):
    layer_count, row_count, col_count = weights.shape
    blocks = weights.reshape(layer_count, row_count // BLOCK, BLOCK, col_count // BLOCK, BLOCK)
    block_max = lax.optimization_barrier(jnp.max(jnp.abs(blocks), axis=(2, 4))).astype(jnp.float32) + 1e-06
    scaled = blocks.astype(jnp.float32) / block_max[:, :, None, :, None]
    return (block_max, scaled.reshape(layer_count, row_count, col_count).astype(jnp.bfloat16))

def key_rows(group_acts, span_begin, key_weight, key_gain):
    feature_count = D // N_TENSOR
    running = jnp.zeros((group_acts.shape[0], key_weight.shape[1]), jnp.float32)
    for quarter in range(N_TENSOR):
        product = jnp.dot(group_acts[:, quarter * feature_count:(quarter + 1) * feature_count], key_weight[quarter * feature_count:(quarter + 1) * feature_count], preferred_element_type=jnp.float32)
        rounded = lax.optimization_barrier(product.astype(jnp.bfloat16))
        running = running + rounded.astype(jnp.float32)
    return finish_keys(running, span_begin, key_gain)

def reference(activations, key_weight, key_gain, span_start, next_weight):
    groups = activations.reshape(N_FSDP, TOK, D)
    keys_all = lax.map(lambda group_item: key_rows(group_item[0], group_item[1], key_weight, key_gain), (groups, span_start))
    new_keys = keys_all.reshape(N_FSDP * TOK, -1)
    block_max, next_scaled = quantize(next_weight)
    return (new_keys, next_scaled, block_max)
```

```python
import functools
import math

import jax
import jax.numpy as jnp
from jax import lax
from jax.experimental import pallas as pl
from jax.experimental.pallas import tpu as pltpu
from jax.sharding import Mesh
from jax.sharding import PartitionSpec as P

BLOCK = 128
AXES = ("y", "xh", "z", "xl", "c")
SIZES = (4, 2, 8, 2, 2)
F32 = jnp.float32
BF16 = jnp.bfloat16
VMEM_LIMIT = 48 * 1024 * 1024


def shift(x, axis, step):
    n = SIZES[AXES.index(axis)]
    return lax.ppermute(x, axis, [(i, (i + step) % n) for i in range(n)])


def call(kernel, out_shape, flops=0, nbytes=0, **kw):
    return pl.pallas_call(
        kernel,
        out_shape=out_shape,
        compiler_params=pltpu.CompilerParams(vmem_limit_bytes=VMEM_LIMIT),
        cost_estimate=pl.CostEstimate(flops=flops, bytes_accessed=nbytes, transcendentals=0),
        **kw,
    )


def project_kernel(idx, a, w, out):
    out[...] = jnp.dot(a[...], w[...], preferred_element_type=F32).astype(out.dtype)


def project_add_kernel(idx, a, w, r, out):
    s = jnp.dot(a[...], w[...], preferred_element_type=F32)
    out[...] = (s + r[...].astype(F32)).astype(out.dtype)


def project_two_kernel(idx, a, w, v, out, own):
    x = a[...]
    out[...] = jnp.dot(x, w[...], preferred_element_type=F32).astype(out.dtype)
    own[...] = jnp.dot(x, v[...], preferred_element_type=F32)


def project(kernel, a, w, tiles, extra, outs, rows=512):
    t, d = a.shape
    width = w.shape[1] // 4
    tile_specs = [
        pl.BlockSpec((d, width), functools.partial(lambda i, idx, k: (0, idx[k]), k=k))
        for k in range(len(tiles))
    ]
    row_spec = pl.BlockSpec((rows, width), lambda i, idx: (i, 0))
    return call(
        kernel,
        [jax.ShapeDtypeStruct((t, width), dt) for dt in outs],
        flops=2 * t * d * width * len(tiles),
        nbytes=2 * t * d + 2 * d * width * len(tiles) + 4 * t * width,
        grid_spec=pltpu.PrefetchScalarGridSpec(
            num_scalar_prefetch=1,
            grid=(t // rows,),
            in_specs=[pl.BlockSpec((rows, d), lambda i, idx: (i, 0))]
            + tile_specs
            + [row_spec] * len(extra),
            out_specs=[row_spec] * len(outs),
        ),
    )(jnp.stack(tiles).astype(jnp.int32), a, *([w] * len(tiles)), *extra)


def finish_kernel(own, r, q, gain, cosine, sine, out):
    g = gain[...]
    c = cosine[...]
    s = sine[...]
    for h in range(2):
        at = slice(h * 128, (h + 1) * 128)
        x = own[:, at] + r[:, at].astype(F32) + q[:, at].astype(F32)
        n = x * lax.rsqrt(jnp.mean(x * x, axis=-1, keepdims=True) + 1e-06) * g
        out[:, at] = (n * c + pltpu.roll(n, 64, 1) * s).astype(BF16)


def finish(own, r, q, gain, cosine, sine, rows=512):
    t, width = own.shape
    wide = pl.BlockSpec((rows, width), lambda i: (i, 0))
    narrow = pl.BlockSpec((rows, 128), lambda i: (i, 0))
    return call(
        finish_kernel,
        jax.ShapeDtypeStruct((t, width), BF16),
        flops=20 * t * width,
        nbytes=16 * t * width,
        grid=(t // rows,),
        in_specs=[wide, wide, wide, pl.BlockSpec((1, 128), lambda i: (0, 0)), narrow, narrow],
        out_specs=wide,
    )(own, r, q, gain.reshape(1, 128), cosine, sine)


def tables(span_begin, t):
    positions = (span_begin + jnp.arange(t, dtype=jnp.int32)).astype(F32)
    lane = jnp.arange(128, dtype=jnp.int32)
    frequency = jnp.exp((lane % 64).astype(F32) * (-2.0 * math.log(1000000.0) / 128))
    angles = positions[:, None] * frequency[None, :]
    sign = jnp.where(lane < 64, -1.0, 1.0).astype(F32)
    return jnp.cos(angles), jnp.sin(angles) * sign[None, :]


def split_kernel(w, out):
    for xh in range(2):
        for t in range(4):
            out[xh * 4 + t] = w[:, :, t * 256 : (t + 1) * 256]


def merge_kernel(x, *outs):
    for layer in range(2):
        for xh in range(2):
            parts = [x[xh * 4 + t, layer].astype(F32) for t in range(4)]
            outs[layer][xh] = jnp.concatenate(parts, axis=0).astype(BF16)


def place_rows_kernel(z, *refs):
    out = refs[-1]
    for d, ref in enumerate(refs[:-1]):
        at = pl.multiple_of(lax.rem(z[0] + d, 8) * 80, 16)
        out[:, pl.ds(at, 80), :] = ref[...]


def place_lead_kernel(y, *refs):
    out = refs[-1]
    for d, ref in enumerate(refs[:-1]):
        out[lax.rem(y[0] + d, 4)] = ref[...]


SMEM = pl.BlockSpec(memory_space=pltpu.SMEM)
VMEM = pl.BlockSpec(memory_space=pltpu.VMEM)


def place(kernel, index, pieces, shape):
    return call(
        kernel,
        jax.ShapeDtypeStruct(shape, BF16),
        nbytes=4 * math.prod(shape),
        in_specs=[SMEM] + [VMEM] * len(pieces),
        out_specs=VMEM,
    )(index, *pieces)


def scale_unit(x, first, put, bm):
    lane = lax.broadcasted_iota(jnp.int32, (1, 128), 1)
    for j in range(2):
        row = bm[j : j + 1, :]
        for k in range(5):
            blk = x[k * 128 : (k + 1) * 128, j * 128 : (j + 1) * 128]
            m = jnp.max(jnp.abs(blk).astype(F32), axis=(0, 1), keepdims=True) + 1e-06
            put(k, j, (blk.astype(F32) * (1.0 / m)).astype(BF16))
            row = jnp.where(lane == first + k, m, row)
        bm[j : j + 1, :] = row


def scale_groups_kernel(units, n, idx, *refs):
    ins, out, bm = refs[:n], refs[-2], refs[-1]
    i = pl.program_id(0)

    @pl.when(i == 0)
    def _():
        bm[...] = refs[n][...]

    for u, (k, xh) in enumerate(units):

        @pl.when(i == u)
        def _(k=k, xh=xh):
            x = ins[k][...] if xh is None else ins[k][xh]

            def put(r, j, v):
                out[0, r * 128 : (r + 1) * 128, j * 128 : (j + 1) * 128] = v

            scale_unit(x, idx[i] * 5, put, bm)


def scale_groups(pieces, groups, bm, buffer):
    units = []
    for k, p in enumerate(pieces):
        units += [(k, None)] if p.ndim == 2 else [(k, xh) for xh in range(p.shape[0])]
    n = len(pieces)
    ins = list(pieces) + [bm]
    in_specs = [
        pl.BlockSpec(p.shape, functools.partial(lambda i, idx, nd: (0,) * nd, nd=p.ndim))
        for p in ins
    ]
    alias = {}
    if buffer is not None:
        ins.append(buffer)
        in_specs.append(pl.BlockSpec(memory_space=pl.ANY))
        alias = {n + 2: 0}
    return call(
        functools.partial(scale_groups_kernel, units, n),
        [jax.ShapeDtypeStruct((2, 5120, 256), BF16), jax.ShapeDtypeStruct((2, 128), F32)],
        flops=len(units) * 640 * 256 * 8,
        nbytes=len(units) * 640 * 256 * 4,
        grid_spec=pltpu.PrefetchScalarGridSpec(
            num_scalar_prefetch=1,
            grid=(len(units),),
            in_specs=in_specs,
            out_specs=[
                pl.BlockSpec((1, 640, 256), lambda i, idx: (0, idx[i], 0)),
                pl.BlockSpec((2, 128), lambda i, idx: (0, 0)),
            ],
        ),
        input_output_aliases=alias,
    )(jnp.stack(groups).astype(jnp.int32), *ins)


def ring_kernel(z, *refs):
    pieces, low, high, bma, _, out, bm, held, acc = (
        refs[:7], refs[7], refs[8], refs[9], refs[10], refs[11], refs[12], refs[13], refs[14]
    )
    i = pl.program_id(0)

    @pl.when(i == 0)
    def _():
        acc[...] = jnp.zeros_like(acc)

    for xh in range(2):
        for d, ref in enumerate(pieces):
            at = pl.multiple_of(lax.rem(z[0] + z[1 + d], 8) * 80, 16)
            held[pl.ds(at, 80), :] = ref[0, xh]
        at = pl.multiple_of(lax.rem(z[0] + 4, 8) * 80, 16)

        @pl.when(i < 2)
        def _():
            held[pl.ds(at, 80), :] = low[0, xh]

        @pl.when(i >= 2)
        def _():
            held[pl.ds(at, 80), :] = high[0, xh]

        def put(r, j, v):
            out[0, xh * 640 + r * 128 : xh * 640 + (r + 1) * 128, j * 128 : (j + 1) * 128] = v

        scale_unit(held, (i * 2 + xh) * 5, put, acc)

    @pl.when(i == 3)
    def _():
        bm[0] = bma[:, :40]
        bm[1] = acc[:, :40]


def scale_ring(z0, pieces, offsets, low, high, bma, buffer):
    whole = pl.BlockSpec((1, 2, 80, 256), lambda i, z: (i, 0, 0, 0))
    return call(
        ring_kernel,
        [jax.ShapeDtypeStruct((2, 5120, 256), BF16), jax.ShapeDtypeStruct((2, 2, 40), F32)],
        flops=5120 * 256 * 8,
        nbytes=5120 * 256 * 4,
        grid_spec=pltpu.PrefetchScalarGridSpec(
            num_scalar_prefetch=1,
            grid=(4,),
            in_specs=[whole] * 7
            + [
                pl.BlockSpec((1, 2, 80, 256), lambda i, z: (jnp.minimum(i, 1), 0, 0, 0)),
                pl.BlockSpec((1, 2, 80, 256), lambda i, z: (jnp.maximum(i - 2, 0), 0, 0, 0)),
                pl.BlockSpec((2, 128), lambda i, z: (0, 0)),
                pl.BlockSpec(memory_space=pl.ANY),
            ],
            out_specs=[
                pl.BlockSpec((1, 1280, 256), lambda i, z: (1, i, 0)),
                pl.BlockSpec((2, 2, 40), lambda i, z: (0, 0, 0)),
            ],
            scratch_shapes=[pltpu.VMEM((640, 256), BF16), pltpu.VMEM((2, 128), F32)],
        ),
        input_output_aliases={11: 0},
    )(jnp.stack([z0] + [jnp.int32(o) for o in offsets]), *pieces, low, high, bma, buffer)


def body(activations, key_weight, key_gain, span_start, next_weight):
    y0, z0 = lax.axis_index("y"), lax.axis_index("z")
    xl, c = lax.axis_index("xl"), lax.axis_index("c")

    spread = call(
        split_kernel,
        jax.ShapeDtypeStruct((8, 2, 20, 256), BF16),
        nbytes=4 * 8 * 2 * 20 * 256,
        in_specs=[VMEM],
        out_specs=VMEM,
    )(next_weight)
    line = lax.all_to_all(spread, ("xh", "xl", "c"), split_axis=0, concat_axis=0, tiled=True)
    a0, b0 = call(
        merge_kernel,
        [jax.ShapeDtypeStruct((2, 80, 256), BF16)] * 2,
        nbytes=4 * 8 * 2 * 20 * 256,
        in_specs=[VMEM],
        out_specs=[VMEM] * 2,
    )(line)

    by = [b0, shift(b0, "y", -1), shift(b0, "y", 2), shift(b0, "y", 1)]
    mb = place(place_lead_kernel, y0.reshape(1), by, (4, 2, 80, 256))
    az = {0: a0}
    for d in (1, 2, 3):
        az[d] = shift(az[d - 1], "z", -1)
        az[8 - d] = shift(az[(9 - d) % 8], "z", 1)
    az[4] = shift(az[3], "z", -1)
    ma = place(place_rows_kernel, z0.reshape(1), [az[d] for d in range(8)], (2, 640, 256))

    bz = {0: mb}
    for d in (1, 2, 3):
        bz[d] = shift(bz[d - 1], "z", -1)
        bz[8 - d] = shift(bz[(9 - d) % 8], "z", 1)
    low = shift(bz[3][:2], "z", -1)
    high = shift(bz[5][2:], "z", 1)

    up, down = shift(ma, "y", -1), shift(ma, "y", 1)
    far0 = shift(up[0], "y", -1)
    far1 = shift(down[1], "y", 1)

    far, near = (1 - xl) * 2, xl * 2
    (p1,) = project(project_kernel, activations, key_weight, [far + 1 - c], [], [BF16])
    r1 = shift(p1, "c", 1)
    (p2,) = project(project_add_kernel, activations, key_weight, [far + c], [r1], [BF16])
    r2 = shift(p2, "xl", 1)
    p3, own = project(
        project_two_kernel, activations, key_weight, [near + 1 - c, near + c], [], [BF16, F32]
    )
    r3 = shift(p3, "c", 1)
    cosine, sine = tables(span_start[0], activations.shape[0])
    new_keys = finish(own, r3, r2, key_gain, cosine, sine)

    g = lambda d: lax.rem(y0 + d, 4) * 2
    bm = jnp.zeros((2, 128), F32)
    buf, bm = scale_groups([ma], [g(0), g(0) + 1], bm, None)
    buf, bm = scale_groups([up, down], [g(1), g(1) + 1, g(3), g(3) + 1], bm, buf)
    buf, bm = scale_groups([far0, far1], [g(2), g(2) + 1], bm, buf)
    order = [0, 1, 7, 2, 6, 3, 5]
    next_scaled, block_max = scale_ring(
        z0, [bz[d] for d in order], order, low, high, bm, buf
    )
    return new_keys, next_scaled, block_max.transpose(0, 2, 1)


def solution(mesh):
    line = Mesh(mesh.devices.reshape(SIZES), AXES)
    fsdp, tensor = ("y", "xh", "z"), ("xl", "c")
    placed = (
        P(fsdp, tensor),
        P(tensor, None),
        P(),
        P(fsdp),
        P(None, fsdp + tensor, None),
    )
    return jax.shard_map(
        body,
        mesh=line,
        in_specs=placed,
        out_specs=(P(fsdp, tensor), P(None, None, tensor), P(None, None, tensor)),
        check_vma=False,
    )
```

```python
import functools
import math

import jax
import jax.numpy as jnp
from jax import lax
from jax.experimental import pallas as pl
from jax.experimental.pallas import tpu as pltpu
from jax.sharding import Mesh
from jax.sharding import PartitionSpec as P

BLOCK = 128
AXES = ("y", "xh", "z", "xl", "c")
SIZES = (4, 2, 8, 2, 2)
F32 = jnp.float32
BF16 = jnp.bfloat16
MIB = 1024 * 1024
NA = 3


after = lax.optimization_barrier


def shift(x, axis, step):
    n = SIZES[AXES.index(axis)]
    return lax.ppermute(x, axis, [(i, (i + step) % n) for i in range(n)])


def call(kernel, out_shape, flops=0, nbytes=0, vmem=16, **kw):
    return pl.pallas_call(
        kernel,
        out_shape=out_shape,
        compiler_params=pltpu.CompilerParams(vmem_limit_bytes=vmem * MIB),
        cost_estimate=pl.CostEstimate(flops=flops, bytes_accessed=nbytes, transcendentals=0),
        **kw,
    )


VMEM = pl.BlockSpec(memory_space=pltpu.VMEM)


def project_kernel(a, w, pair, mid, own, av, wv, asem, wsem):
    n, rows = av.shape[0], av.shape[1]
    xl, c = lax.axis_index("xl"), lax.axis_index("c")
    tiles = [3 - 2 * xl - c, 2 * xl + 1 - c, 2 - 2 * xl + c, 2 * xl + c]

    def get_w(k):
        at = pl.multiple_of(tiles[k] * 256, 256)
        return pltpu.make_async_copy(w.at[:, pl.ds(at, 256)], wv.at[k], wsem.at[k])

    def get_a(i):
        return pltpu.make_async_copy(a.at[pl.ds(i * rows, rows), :], av.at[i], asem.at[i])

    get_a(0).start()
    for k in range(4):
        get_w(k).start()
    for i in range(1, n):
        get_a(i).start()
    for i in range(n):
        get_a(i).wait()
        at = slice(i * rows, (i + 1) * rows)
        for k, (out, col) in enumerate([(pair, 0), (pair, 256), (mid, 0), (own, 0)]):
            if i == 0:
                get_w(k).wait()
            p = jnp.dot(av[i], wv[k], preferred_element_type=F32)
            out[at, col : col + 256] = p.astype(BF16)


def project(a, w, n=NA):
    t, d = a.shape
    width = w.shape[1] // 4
    hbm = pl.BlockSpec(memory_space=pltpu.HBM)
    return call(
        project_kernel,
        [jax.ShapeDtypeStruct((t, k * width), BF16) for k in (2, 1, 1)],
        flops=8 * t * d * width,
        nbytes=2 * t * d + 8 * d * width + 8 * t * width,
        vmem=58,
        in_specs=[hbm, hbm],
        out_specs=[VMEM] * 3,
        scratch_shapes=[
            pltpu.VMEM((n, t // n, d), BF16),
            pltpu.VMEM((4, d, width), BF16),
            pltpu.SemaphoreType.DMA((n,)),
            pltpu.SemaphoreType.DMA((4,)),
        ],
    )(a, w)


def add_kernel(x, r, out):
    out[...] = (x[...].astype(F32) + r[...].astype(F32)).astype(BF16)


def add(x, r, rows=768):
    t, width = x.shape
    spec = pl.BlockSpec((rows, width), lambda i: (i, 0))
    return call(
        add_kernel,
        jax.ShapeDtypeStruct((t, width), BF16),
        flops=t * width,
        nbytes=6 * t * width,
        grid=(t // rows,),
        in_specs=[spec, pl.BlockSpec((rows, width), lambda i: (i, 0))],
        out_specs=spec,
    )(x, r)


def finish_kernel(own, r1, r2, gain, cosine, sine, out):
    g = gain[...]
    c = cosine[...]
    s = sine[...]
    for h in range(2):
        at = slice(h * 128, (h + 1) * 128)
        x = own[:, at].astype(F32) + r1[:, at].astype(F32) + r2[:, at].astype(F32)
        n = x * lax.rsqrt(jnp.mean(x * x, axis=-1, keepdims=True) + 1e-06) * g
        out[:, at] = (n * c + pltpu.roll(n, 64, 1) * s).astype(BF16)


def finish(own, r1, r2, gain, cosine, sine, rows=768):
    t, width = own.shape
    wide = pl.BlockSpec((rows, width), lambda i: (i, 0))
    narrow = pl.BlockSpec((rows, 128), lambda i: (i, 0))
    return call(
        finish_kernel,
        jax.ShapeDtypeStruct((t, width), BF16),
        flops=20 * t * width,
        nbytes=14 * t * width,
        grid=(t // rows,),
        in_specs=[wide, pl.BlockSpec((rows, width), lambda i: (i, 1)), wide]
        + [pl.BlockSpec((1, 128), lambda i: (0, 0)), narrow, narrow],
        out_specs=wide,
    )(own, r1, r2, gain.reshape(1, 128), cosine, sine)


def tables(span_begin, t):
    lane = jnp.arange(128, dtype=jnp.int32)
    frequency = jnp.exp((lane % 64).astype(F32) * (-2.0 * math.log(1000000.0) / 128))
    k = jnp.arange(t // 32 + 32, dtype=jnp.int32)
    steps = jnp.where(k < t // 32, span_begin + 32 * k, k - t // 32)
    angles = steps.astype(F32)[:, None] * frequency[None, :]
    sign = jnp.where(lane < 64, -1.0, 1.0).astype(F32)
    c, s = lax.optimization_barrier((jnp.cos(angles), jnp.sin(angles)))
    ca, sa = c[: t // 32, None, :], s[: t // 32, None, :]
    cb, sb = c[None, t // 32 :, :], s[None, t // 32 :, :]
    cosine = ca * cb - sa * sb
    sine = (sa * cb + ca * sb) * sign
    return cosine.reshape(t, 128), sine.reshape(t, 128)


def spread_kernel(w, out):
    x = w[...].astype(F32)
    rows = jnp.concatenate([x[:, 0, :], x[:, 1, :]], axis=0).astype(BF16)
    for xh in range(2):
        for t in range(4):
            out[xh * 4 + t] = rows[:, t * 256 : (t + 1) * 256]


def merge_kernel(x, outa, outb):
    for xh in range(2):
        lines = [x[xh * 4 + t].astype(F32) for t in range(4)]
        for layer, out in enumerate((outa, outb)):
            parts = [line[layer * 20 : layer * 20 + 20] for line in lines]
            out[xh * 80 : xh * 80 + 80, :] = jnp.concatenate(parts, axis=0).astype(BF16)


def stack_kernel(*refs):
    y = lax.axis_index("y")
    out = refs[-1]
    for d in range(4):
        at = pl.multiple_of(lax.rem(y + d, 4) * 160, 16)
        out[pl.ds(at, 160), :] = refs[d][...]


def rows_kernel(*refs):
    z = lax.axis_index("z")
    out = refs[-1]
    for h in range(2):
        for d in range(8):
            at = pl.multiple_of(lax.rem(z + d, 8) * 80 + h * 640, 16)
            out[pl.ds(at, 80), :] = refs[d][h * 80 : h * 80 + 80, :]


def small(kernel, shapes, *arrays):
    single = len(shapes) == 1
    out = [jax.ShapeDtypeStruct(s, BF16) for s in shapes]
    return call(
        kernel,
        out[0] if single else out,
        nbytes=4 * sum(math.prod(s) for s in shapes),
        in_specs=[VMEM] * len(arrays),
        out_specs=VMEM if single else [VMEM] * len(out),
    )(*arrays)


def scale_blocks(x, first, put, bm):
    lane = lax.broadcasted_iota(jnp.int32, (1, 128), 1)
    for j in range(2):
        row = bm[j : j + 1, :]
        for k in range(x.shape[0] // 128):
            blk = x[k * 128 : (k + 1) * 128, j * 128 : (j + 1) * 128]
            top = jnp.max(jnp.abs(blk), axis=0, keepdims=True).astype(F32)
            m = jnp.max(top, axis=1, keepdims=True) + 1e-06
            put(k, j, (blk.astype(F32) * (1.0 / m)).astype(BF16))
            row = jnp.where(lane == first + k, m, row)
        bm[j : j + 1, :] = row


def y_at(offsets, i):
    d = offsets[0]
    for u, other in enumerate(offsets[1:], 1):
        d = jnp.where(i == u, other, d)
    return lax.rem(lax.axis_index("y") + d, 4)


def scale_groups_kernel(groups, offsets, n, *refs):
    ins, out, bm = refs[:n], refs[-2], refs[-1]
    i = pl.program_id(0)
    y = lax.axis_index("y")

    @pl.when(i == 0)
    def _():
        bm[...] = refs[n][...] if len(refs) > n + 2 else jnp.zeros_like(bm)

    for u, group in enumerate(groups):

        @pl.when(i == u)
        def _(u=u, group=group):
            row = 0
            for k in group:
                base = row

                def put(r, j, v):
                    out[0, base + r * 128 : base + (r + 1) * 128, j * 128 : (j + 1) * 128] = v

                first = lax.rem(y + offsets[u], 4) * 10 + row // 128
                scale_blocks(ins[k], first, put, bm)
                row += ins[k].shape[0]


def scale_groups(pieces, groups, offsets, done=None):
    n = len(pieces)
    ins = list(pieces)
    alias = {}
    if done is not None:
        ins += [done[1], done[0]]
        alias = {n + 1: 0, n: 1}
    in_specs = [pl.BlockSpec(p.shape, lambda i: (0, 0)) for p in ins[: n + 1]]
    if done is not None:
        in_specs.append(pl.BlockSpec(memory_space=pl.ANY))
    return call(
        functools.partial(scale_groups_kernel, groups, offsets, n),
        [jax.ShapeDtypeStruct((2, 5120, 256), BF16), jax.ShapeDtypeStruct((2, 128), F32)],
        flops=len(groups) * 1280 * 256 * 8,
        nbytes=len(groups) * 1280 * 256 * 4,
        grid=(len(groups),),
        in_specs=in_specs,
        out_specs=[
            pl.BlockSpec((1, 1280, 256), lambda i: (0, y_at(offsets, i), 0)),
            pl.BlockSpec((2, 128), lambda i: (0, 0)),
        ],
        input_output_aliases=alias,
    )(*ins)


def scale_ring_kernel(*refs):
    z = lax.axis_index("z")
    offsets = (0, 1, 2, 3, 5, 6, 7)
    low, high, bma, _, out, bm, held, acc = refs[7:]
    i = pl.program_id(0)

    def place(d, ref):
        for xh in range(2):
            at = pl.multiple_of(lax.rem(z + d, 8) * 80 + xh * 640, 16)
            held[pl.ds(at, 80), :] = ref[xh * 80 : xh * 80 + 80, :]

    @pl.when(i == 0)
    def _():
        acc[...] = jnp.zeros_like(acc)

    for d, ref in zip(offsets, refs[:7]):
        place(d, ref)

    @pl.when(i < 2)
    def _():
        place(4, low)

    @pl.when(i >= 2)
    def _():
        place(4, high)

    def put(r, j, v):
        out[0, r * 128 : (r + 1) * 128, j * 128 : (j + 1) * 128] = v

    scale_blocks(held, i * 10, put, acc)

    @pl.when(i == 3)
    def _():
        bm[0] = bma[:, :40]
        bm[1] = acc[:, :40]


def scale_ring(pieces, low, high, done):
    part = (160, 256)
    return call(
        scale_ring_kernel,
        [jax.ShapeDtypeStruct((2, 5120, 256), BF16), jax.ShapeDtypeStruct((2, 2, 40), F32)],
        flops=5120 * 256 * 8,
        nbytes=5120 * 256 * 4,
        grid=(4,),
        in_specs=[pl.BlockSpec(part, lambda i: (i, 0))] * 7
        + [
            pl.BlockSpec(part, lambda i: (jnp.minimum(i, 1), 0)),
            pl.BlockSpec(part, lambda i: (jnp.maximum(i - 2, 0), 0)),
            pl.BlockSpec((2, 128), lambda i: (0, 0)),
            pl.BlockSpec(memory_space=pl.ANY),
        ],
        out_specs=[
            pl.BlockSpec((1, 1280, 256), lambda i: (1, i, 0)),
            pl.BlockSpec((2, 2, 40), lambda i: (0, 0, 0)),
        ],
        scratch_shapes=[pltpu.VMEM((1280, 256), BF16), pltpu.VMEM((2, 128), F32)],
        input_output_aliases={10: 0},
    )(*pieces, low, high, done[1], done[0])


def body(activations, key_weight, key_gain, span_start, next_weight):
    line = small(spread_kernel, [(8, 40, 256)], next_weight.transpose(1, 0, 2))
    line = lax.all_to_all(line, ("xh", "xl", "c"), split_axis=0, concat_axis=0, tiled=True)
    pair, mid, own = project(activations, key_weight)
    line, pair = after((line, pair))
    a0, b0 = small(merge_kernel, [(160, 256)] * 2, line)

    az = {0: a0}
    az[1], az[7] = shift(a0, "z", -1), shift(a0, "z", 1)
    r1 = shift(pair, "c", 1)
    half = add(mid, r1)
    az[1], az[7], half, b0 = after((az[1], az[7], half, b0))
    r2 = shift(half, "xl", 1)
    az[2], az[6] = shift(az[1], "z", -1), shift(az[7], "z", 1)
    by = [b0, shift(b0, "y", -1), shift(b0, "y", 2), shift(b0, "y", 1)]
    az[3], az[5] = shift(az[2], "z", -1), shift(az[6], "z", 1)
    az[4] = shift(az[3], "z", -1)
    mb = small(stack_kernel, [(640, 256)], *by)
    ma = small(rows_kernel, [(1280, 256)], *[az[d] for d in range(8)])

    mb, ma = after((mb, ma))

    bz = {0: mb}
    bz[1], bz[7] = shift(mb, "z", -1), shift(mb, "z", 1)
    bz[1], bz[7], r2 = after((bz[1], bz[7], r2))
    up, down = shift(ma, "y", -1), shift(ma, "y", 1)
    done = scale_groups([ma], [(0,)], [0])
    bz[2], bz[6] = shift(bz[1], "z", -1), shift(bz[7], "z", 1)
    bz[2], bz[6], *done = after((bz[2], bz[6], *done))
    bz[3], bz[5] = shift(bz[2], "z", -1), shift(bz[6], "z", 1)
    far0 = shift(up[:640], "y", -1)
    far1 = shift(down[640:], "y", 1)
    cosine, sine = tables(span_start[0], activations.shape[0])
    new_keys = finish(own, r1, r2, key_gain, cosine, sine)
    done = scale_groups([up, down], [(0,), (1,)], [1, 3], done)
    bz[3], bz[5], new_keys, *done = after((bz[3], bz[5], new_keys, *done))
    low = shift(bz[3][:320], "z", -1)
    high = shift(bz[5][320:], "z", 1)
    done = scale_groups([far0, far1], [(0, 1)], [2], done)
    low, high, *done = after((low, high, *done))
    pieces = [bz[d] for d in (0, 1, 2, 3, 5, 6, 7)]
    next_scaled, block_max = scale_ring(pieces, low, high, done)
    return new_keys, next_scaled, block_max.transpose(0, 2, 1)


def solution(mesh):
    line = Mesh(mesh.devices.reshape(SIZES), AXES)
    fsdp, tensor = ("y", "xh", "z"), ("xl", "c")
    placed = (
        P(fsdp, tensor),
        P(tensor, None),
        P(),
        P(fsdp),
        P(None, fsdp + tensor, None),
    )
    return jax.shard_map(
        body,
        mesh=line,
        in_specs=placed,
        out_specs=(P(fsdp, tensor), P(None, None, tensor), P(None, None, tensor)),
        check_vma=False,
    )
```

```python
import functools
import math

import jax
import jax.numpy as jnp
from jax import lax
from jax.experimental import pallas as pl
from jax.experimental.pallas import tpu as pltpu
from jax.sharding import Mesh
from jax.sharding import PartitionSpec as P

BLOCK = 128
AXES = ("yh", "yl", "xh", "z", "xl", "c")
SIZES = (2, 2, 2, 8, 2, 2)
Y = ("yh", "yl")
F32 = jnp.float32
BF16 = jnp.bfloat16
MIB = 1024 * 1024
NA = 3


after = lax.optimization_barrier


def shift(x, axis, step):
    n = 4 if axis == Y else SIZES[AXES.index(axis)]
    return lax.ppermute(x, axis, [(i, (i + step) % n) for i in range(n)])


def call(kernel, out_shape, flops=0, nbytes=0, vmem=16, **kw):
    return pl.pallas_call(
        kernel,
        out_shape=out_shape,
        compiler_params=pltpu.CompilerParams(vmem_limit_bytes=vmem * MIB),
        cost_estimate=pl.CostEstimate(flops=flops, bytes_accessed=nbytes, transcendentals=0),
        **kw,
    )


VMEM = pl.BlockSpec(memory_space=pltpu.VMEM)


def project_kernel(a, w, pair, mid, own, av, wv, asem, wsem):
    n, rows = av.shape[0], av.shape[1]
    xl, c = lax.axis_index("xl"), lax.axis_index("c")
    tiles = [3 - 2 * xl - c, 2 * xl + 1 - c, 2 - 2 * xl + c, 2 * xl + c]

    def get_w(k):
        at = pl.multiple_of(tiles[k] * 256, 256)
        return pltpu.make_async_copy(w.at[:, pl.ds(at, 256)], wv.at[k], wsem.at[k])

    def get_a(i):
        return pltpu.make_async_copy(a.at[pl.ds(i * rows, rows), :], av.at[i], asem.at[i])

    get_a(0).start()
    for k in range(4):
        get_w(k).start()
    for i in range(1, n):
        get_a(i).start()
    for i in range(n):
        get_a(i).wait()
        at = slice(i * rows, (i + 1) * rows)
        for k, (out, col) in enumerate([(pair, 0), (pair, 256), (mid, 0), (own, 0)]):
            if i == 0:
                get_w(k).wait()
            p = jnp.dot(av[i], wv[k], preferred_element_type=F32)
            out[at, col : col + 256] = p.astype(BF16)


def project(a, w, n=NA):
    t, d = a.shape
    width = w.shape[1] // 4
    hbm = pl.BlockSpec(memory_space=pltpu.HBM)
    return call(
        project_kernel,
        [jax.ShapeDtypeStruct((t, k * width), BF16) for k in (2, 1, 1)],
        flops=8 * t * d * width,
        nbytes=2 * t * d + 8 * d * width + 8 * t * width,
        vmem=58,
        in_specs=[hbm, hbm],
        out_specs=[VMEM] * 3,
        scratch_shapes=[
            pltpu.VMEM((n, t // n, d), BF16),
            pltpu.VMEM((4, d, width), BF16),
            pltpu.SemaphoreType.DMA((n,)),
            pltpu.SemaphoreType.DMA((4,)),
        ],
    )(a, w)


def add_kernel(x, r, out):
    out[...] = (x[...].astype(F32) + r[...].astype(F32)).astype(BF16)


def add(x, r, rows=768):
    t, width = x.shape
    spec = pl.BlockSpec((rows, width), lambda i: (i, 0))
    return call(
        add_kernel,
        jax.ShapeDtypeStruct((t, width), BF16),
        flops=t * width,
        nbytes=6 * t * width,
        grid=(t // rows,),
        in_specs=[spec, pl.BlockSpec((rows, width), lambda i: (i, 0))],
        out_specs=spec,
    )(x, r)


def finish_kernel(own, r1, r2, gain, cosine, sine, out):
    g = gain[...]
    c = cosine[...]
    s = sine[...]
    for h in range(2):
        at = slice(h * 128, (h + 1) * 128)
        x = own[:, at].astype(F32) + r1[:, at].astype(F32) + r2[:, at].astype(F32)
        n = x * lax.rsqrt(jnp.mean(x * x, axis=-1, keepdims=True) + 1e-06) * g
        out[:, at] = (n * c + pltpu.roll(n, 64, 1) * s).astype(BF16)


def finish(own, r1, r2, gain, cosine, sine, rows=768):
    t, width = own.shape
    wide = pl.BlockSpec((rows, width), lambda i: (i, 0))
    narrow = pl.BlockSpec((rows, 128), lambda i: (i, 0))
    return call(
        finish_kernel,
        jax.ShapeDtypeStruct((t, width), BF16),
        flops=20 * t * width,
        nbytes=14 * t * width,
        grid=(t // rows,),
        in_specs=[wide, pl.BlockSpec((rows, width), lambda i: (i, 1)), wide]
        + [pl.BlockSpec((1, 128), lambda i: (0, 0)), narrow, narrow],
        out_specs=wide,
    )(own, r1, r2, gain.reshape(1, 128), cosine, sine)


def tables(span_begin, t):
    lane = jnp.arange(128, dtype=jnp.int32)
    frequency = jnp.exp((lane % 64).astype(F32) * (-2.0 * math.log(1000000.0) / 128))
    k = jnp.arange(t // 32 + 32, dtype=jnp.int32)
    steps = jnp.where(k < t // 32, span_begin + 32 * k, k - t // 32)
    angles = steps.astype(F32)[:, None] * frequency[None, :]
    sign = jnp.where(lane < 64, -1.0, 1.0).astype(F32)
    c, s = lax.optimization_barrier((jnp.cos(angles), jnp.sin(angles)))
    ca, sa = c[: t // 32, None, :], s[: t // 32, None, :]
    cb, sb = c[None, t // 32 :, :], s[None, t // 32 :, :]
    cosine = ca * cb - sa * sb
    sine = (sa * cb + ca * sb) * sign
    return cosine.reshape(t, 128), sine.reshape(t, 128)


def spread_kernel(w, out):
    x = w[...].astype(F32)
    rows = jnp.concatenate([x[:, 0, :], x[:, 1, :]], axis=0).astype(BF16)
    for k in range(4):
        for t in range(4):
            out[k * 4 + t] = rows[:, t * 256 : (t + 1) * 256]


def fold(x):
    wide = jnp.concatenate([x[:40], x[40:]], axis=1)
    return jnp.concatenate([wide, jnp.zeros((8, 256), F32)], axis=0)


def unfold(x):
    return jnp.concatenate([x[:40, :128], x[:40, 128:]], axis=0)


def merge_kernel(x, outa, outb):
    mine = lax.axis_index("yl") * 8
    for xh in range(2):
        lines = [x[mine + xh * 4 + t].astype(F32) for t in range(4)]
        one, two = (
            jnp.concatenate([line[k * 20 : k * 20 + 20] for line in lines], axis=0)
            for k in range(2)
        )
        outa[xh * 80 : xh * 80 + 80, :] = one.astype(BF16)
        if xh == 1:
            outa[160:208, :] = fold(two[:, 128:]).astype(BF16)
    for yl in range(2):
        for xh in range(2):
            lines = [x[yl * 8 + xh * 4 + t].astype(F32) for t in range(4)]
            two = jnp.concatenate([line[20:40] for line in lines], axis=0)
            if xh == 0:
                outb[yl * 128 : yl * 128 + 80, :] = two.astype(BF16)
            else:
                outb[yl * 128 + 80 : yl * 128 + 128, :] = fold(two[:, :128]).astype(BF16)


def stack_kernel(own, other, out):
    yh = lax.axis_index("yh")
    for d, ref in enumerate((own, other)):
        for yl in range(2):
            at = lax.rem(yh + d, 2) * 2 + yl
            out[pl.ds(pl.multiple_of(at * 80, 16), 80), :] = ref[yl * 128 : yl * 128 + 80, :]
            col = pl.multiple_of(at // 2 * 128, 128)
            side = unfold(ref[yl * 128 + 80 : yl * 128 + 128, :].astype(F32))
            out[320 + yl * 80 : 400 + yl * 80, pl.ds(col, 128)] = side.astype(BF16)


def rows_kernel(*refs):
    z = lax.axis_index("z")
    out = refs[-1]
    for d in range(8):
        at = lax.rem(z + d, 8)
        for h in range(2):
            row = pl.multiple_of(320 + at * 80 + h * 640, 16)
            out[pl.ds(row, 80), :] = refs[d][h * 80 : h * 80 + 80, :]
        row = pl.multiple_of(lax.rem(at, 4) * 80, 16)
        col = pl.multiple_of(at // 4 * 128, 128)
        out[pl.ds(row, 80), pl.ds(col, 128)] = unfold(refs[d][160:208, :].astype(F32)).astype(BF16)


def small(kernel, shapes, *arrays):
    single = len(shapes) == 1
    out = [jax.ShapeDtypeStruct(s, BF16) for s in shapes]
    return call(
        kernel,
        out[0] if single else out,
        nbytes=4 * sum(math.prod(s) for s in shapes),
        in_specs=[VMEM] * len(arrays),
        out_specs=VMEM if single else [VMEM] * len(out),
    )(*arrays)


def scale_blocks(x, start, count, first, put, bm):
    lane = lax.broadcasted_iota(jnp.int32, (1, 128), 1)
    for j in range(2):
        row = bm[j : j + 1, :]
        for k in range(count // 128):
            blk = x[start + k * 128 : start + (k + 1) * 128, j * 128 : (j + 1) * 128]
            top = jnp.max(jnp.abs(blk), axis=0, keepdims=True).astype(F32)
            m = jnp.max(top, axis=1, keepdims=True) + 1e-06
            put(k, j, (blk.astype(F32) * (1.0 / m)).astype(BF16))
            row = jnp.where(lane == first + k, m, row)
        bm[j : j + 1, :] = row


def y_at(offsets, i):
    d = offsets[0]
    for u, other in enumerate(offsets[1:], 1):
        d = jnp.where(i == u, other, d)
    return lax.rem(lax.axis_index(Y) + d, 4)


def scale_groups_kernel(groups, offsets, n, *refs):
    ins, out, bm = refs[:n], refs[-2], refs[-1]
    i = pl.program_id(0)
    y = lax.axis_index(Y)

    @pl.when(i == 0)
    def _():
        bm[...] = refs[n][...] if len(refs) > n + 2 else jnp.zeros_like(bm)

    for u, group in enumerate(groups):

        @pl.when(i == u)
        def _(u=u, group=group):
            row = 0
            for k, start, count in group:
                base = row

                def put(r, j, v):
                    out[0, base + r * 128 : base + (r + 1) * 128, j * 128 : (j + 1) * 128] = v

                first = lax.rem(y + offsets[u], 4) * 10 + row // 128
                scale_blocks(ins[k], start, count, first, put, bm)
                row += count


def scale_groups(pieces, groups, offsets, done=None):
    n = len(pieces)
    ins = list(pieces)
    alias = {}
    if done is not None:
        ins += [done[1], done[0]]
        alias = {n + 1: 0, n: 1}
    in_specs = [pl.BlockSpec(p.shape, lambda i: (0, 0)) for p in ins[: n + 1]]
    if done is not None:
        in_specs.append(pl.BlockSpec(memory_space=pl.ANY))
    return call(
        functools.partial(scale_groups_kernel, groups, offsets, n),
        [jax.ShapeDtypeStruct((2, 5120, 256), BF16), jax.ShapeDtypeStruct((2, 128), F32)],
        flops=len(groups) * 1280 * 256 * 8,
        nbytes=len(groups) * 1280 * 256 * 4,
        grid=(len(groups),),
        in_specs=in_specs,
        out_specs=[
            pl.BlockSpec((1, 1280, 256), lambda i: (0, y_at(offsets, i), 0)),
            pl.BlockSpec((2, 128), lambda i: (0, 0)),
        ],
        input_output_aliases=alias,
    )(*ins)


def scale_ring_kernel(*refs):
    z, y = lax.axis_index("z"), lax.axis_index(Y)
    whole, half, low, high, part, extra = refs[:7], refs[7:14], *refs[14:17], refs[17:21]
    bma, _, out, bm, held, acc = refs[21:]
    i = pl.program_id(0)
    col = pl.multiple_of(i // 2 * 128, 128)

    @pl.when(i == 0)
    def _():
        acc[...] = jnp.zeros_like(acc)

    def row(d):
        return pl.multiple_of(lax.rem(z + d, 8) * 80, 16)

    def place(d, ref):
        held[pl.ds(row(d), 80), :] = ref[...]

    for d, ref, side in zip((0, 1, 2, 3, 5, 6, 7), whole, half):
        place(d, ref)
        held[pl.ds(row(d) + 640, 80), 0:128] = side[:, pl.ds(col, 128)]
    held[pl.ds(row(4) + 640, 80), 0:128] = part[:, pl.ds(col, 128)]

    @pl.when(i < 3)
    def _():
        place(4, low)

    @pl.when(i == 3)
    def _():
        place(4, high)

    for d, ref in enumerate(extra):

        @pl.when(lax.rem(y + d, 4) == i)
        def _(ref=ref):
            held[640:960, 128:256] = ref[:, 0:128]
            held[960:1280, 128:256] = ref[:, 128:256]

    def put(r, j, v):
        out[0, r * 128 : (r + 1) * 128, j * 128 : (j + 1) * 128] = v

    scale_blocks(held, 0, 1280, i * 10, put, acc)

    @pl.when(i == 3)
    def _():
        bm[0] = bma[:, :40]
        bm[1] = acc[:, :40]


def scale_ring(pieces, low, high, extra, done):
    part = (80, 256)
    return call(
        scale_ring_kernel,
        [jax.ShapeDtypeStruct((2, 5120, 256), BF16), jax.ShapeDtypeStruct((2, 2, 40), F32)],
        flops=5120 * 256 * 8,
        nbytes=5120 * 256 * 4,
        grid=(4,),
        in_specs=[pl.BlockSpec(part, lambda i: (i, 0))] * 7
        + [pl.BlockSpec(part, lambda i: (4 + lax.rem(i, 2), 0))] * 7
        + [
            pl.BlockSpec(part, lambda i: (jnp.minimum(i, 2), 0)),
            pl.BlockSpec(part, lambda i: (0, 0)),
            pl.BlockSpec(part, lambda i: (1 + lax.rem(i, 2), 0)),
        ]
        + [pl.BlockSpec((320, 256), lambda i: (0, 0))] * 4
        + [
            pl.BlockSpec((2, 128), lambda i: (0, 0)),
            pl.BlockSpec(memory_space=pl.ANY),
        ],
        out_specs=[
            pl.BlockSpec((1, 1280, 256), lambda i: (1, i, 0)),
            pl.BlockSpec((2, 2, 40), lambda i: (0, 0, 0)),
        ],
        scratch_shapes=[pltpu.VMEM((1280, 256), BF16), pltpu.VMEM((2, 128), F32)],
        input_output_aliases={22: 0},
    )(*pieces, *pieces, low, high, high, *extra, done[1], done[0])


def body(activations, key_weight, key_gain, span_start, next_weight):
    line = small(spread_kernel, [(16, 40, 256)], next_weight.transpose(1, 0, 2))
    line = lax.all_to_all(line, ("yl", "xh", "xl", "c"), split_axis=0, concat_axis=0, tiled=True)
    pair, mid, own = project(activations, key_weight)
    line, pair = after((line, pair))
    a0, b0 = small(merge_kernel, [(208, 256), (256, 256)], line)

    az = {0: a0}
    az[1], az[7] = shift(a0, "z", -1), shift(a0, "z", 1)
    other = shift(b0, "yh", 1)
    az[2], az[6] = shift(az[1], "z", -1), shift(az[7], "z", 1)
    az[3], az[5] = shift(az[2], "z", -1), shift(az[6], "z", 1)
    az[4] = shift(az[3], "z", -1)
    mb = small(stack_kernel, [(480, 256)], b0, other)
    ma = small(rows_kernel, [(1600, 256)], *[az[d] for d in range(8)])
    mb, ma, pair = after((mb, ma, pair))

    bz = {0: mb}
    bz[1], bz[7] = shift(mb, "z", -1), shift(mb, "z", 1)
    up, down = shift(ma, Y, -1), shift(ma, Y, 1)
    r1 = shift(pair, "c", 1)
    half = add(mid, r1)
    bz[1], bz[7], half = after((bz[1], bz[7], half))
    r2 = shift(half, "xl", 1)
    bz[2], bz[6] = shift(bz[1], "z", -1), shift(bz[7], "z", 1)
    done = scale_groups([ma], [[(0, 320, 1280)]], [0])
    bz[2], bz[6], *done = after((bz[2], bz[6], *done))
    bz[3], bz[5] = shift(bz[2], "z", -1), shift(bz[6], "z", 1)
    far0 = shift(up[:704], Y, -1)
    far1 = shift(down[704:], Y, 1)
    done = scale_groups([up, down], [[(0, 320, 1280)], [(1, 320, 1280)]], [1, 3], done)
    bz[3], bz[5], *done = after((bz[3], bz[5], *done))
    low = shift(bz[3][:240], "z", -1)
    high = shift(bz[5][240:], "z", 1)
    cosine, sine = tables(span_start[0], activations.shape[0])
    new_keys = finish(own, r1, r2, key_gain, cosine, sine)
    far0, far1, new_keys = after((far0, far1, new_keys))
    done = scale_groups([far0, far1], [[(0, 320, 384), (1, 0, 896)]], [2], done)
    low, high, *done = after((low, high, *done))
    pieces = [bz[d] for d in (0, 1, 2, 3, 5, 6, 7)]
    next_scaled, block_max = scale_ring(pieces, low, high, [ma, up, far0, down], done)
    return new_keys, next_scaled, block_max.transpose(0, 2, 1)


def solution(mesh):
    line = Mesh(mesh.devices.reshape(SIZES), AXES)
    fsdp, tensor = (*Y, "xh", "z"), ("xl", "c")
    placed = (
        P(fsdp, tensor),
        P(tensor, None),
        P(),
        P(fsdp),
        P(None, fsdp + tensor, None),
    )
    return jax.shard_map(
        body,
        mesh=line,
        in_specs=placed,
        out_specs=(P(fsdp, tensor), P(None, None, tensor), P(None, None, tensor)),
        check_vma=False,
    )
```

```python
import functools
import math

import jax
import jax.numpy as jnp
from jax import lax
from jax.experimental import pallas as pl
from jax.experimental.pallas import tpu as pltpu
from jax.sharding import Mesh
from jax.sharding import PartitionSpec as P

BLOCK = 128
AXES = ("yh", "yl", "xh", "z", "xl", "c")
SIZES = (2, 2, 2, 8, 2, 2)
Y = ("yh", "yl")
F32 = jnp.float32
BF16 = jnp.bfloat16
MIB = 1024 * 1024
NA = 3


after = lax.optimization_barrier


def shift(x, axis, step):
    n = 4 if axis == Y else SIZES[AXES.index(axis)]
    return lax.ppermute(x, axis, [(i, (i + step) % n) for i in range(n)])


def call(kernel, out_shape, flops=0, nbytes=0, vmem=16, **kw):
    return pl.pallas_call(
        kernel,
        out_shape=out_shape,
        compiler_params=pltpu.CompilerParams(vmem_limit_bytes=vmem * MIB),
        cost_estimate=pl.CostEstimate(flops=flops, bytes_accessed=nbytes, transcendentals=0),
        **kw,
    )


VMEM = pl.BlockSpec(memory_space=pltpu.VMEM)


def project_kernel(a, w, pair, mid, own, av, wv, asem, wsem):
    n, rows = av.shape[0], av.shape[1]
    xl, c = lax.axis_index("xl"), lax.axis_index("c")
    tiles = [3 - 2 * xl - c, 2 * xl + 1 - c, 2 - 2 * xl + c, 2 * xl + c]

    def get_w(k):
        at = pl.multiple_of(tiles[k] * 256, 256)
        return pltpu.make_async_copy(w.at[:, pl.ds(at, 256)], wv.at[k], wsem.at[k])

    def get_a(i):
        return pltpu.make_async_copy(a.at[pl.ds(i * rows, rows), :], av.at[i], asem.at[i])

    get_a(0).start()
    for k in range(4):
        get_w(k).start()
    for i in range(1, n):
        get_a(i).start()
    for i in range(n):
        get_a(i).wait()
        at = slice(i * rows, (i + 1) * rows)
        for k, (out, col) in enumerate([(pair, 0), (pair, 256), (mid, 0), (own, 0)]):
            if i == 0:
                get_w(k).wait()
            p = jnp.dot(av[i], wv[k], preferred_element_type=F32)
            out[at, col : col + 256] = p.astype(BF16)


def project(a, w, n=NA):
    t, d = a.shape
    width = w.shape[1] // 4
    hbm = pl.BlockSpec(memory_space=pltpu.HBM)
    return call(
        project_kernel,
        [jax.ShapeDtypeStruct((t, k * width), BF16) for k in (2, 1, 1)],
        flops=8 * t * d * width,
        nbytes=2 * t * d + 8 * d * width + 8 * t * width,
        vmem=58,
        in_specs=[hbm, hbm],
        out_specs=[VMEM] * 3,
        scratch_shapes=[
            pltpu.VMEM((n, t // n, d), BF16),
            pltpu.VMEM((4, d, width), BF16),
            pltpu.SemaphoreType.DMA((n,)),
            pltpu.SemaphoreType.DMA((4,)),
        ],
    )(a, w)


def add_kernel(x, r, out):
    out[...] = (x[...].astype(F32) + r[...].astype(F32)).astype(BF16)


def add(x, r, rows=768):
    t, width = x.shape
    spec = pl.BlockSpec((rows, width), lambda i: (i, 0))
    return call(
        add_kernel,
        jax.ShapeDtypeStruct((t, width), BF16),
        flops=t * width,
        nbytes=6 * t * width,
        grid=(t // rows,),
        in_specs=[spec, pl.BlockSpec((rows, width), lambda i: (i, 0))],
        out_specs=spec,
    )(x, r)


def finish_kernel(own, r1, r2, gain, cosine, sine, out):
    g = gain[...]
    c = cosine[...]
    s = sine[...]
    for h in range(2):
        at = slice(h * 128, (h + 1) * 128)
        x = own[:, at].astype(F32) + r1[:, at].astype(F32) + r2[:, at].astype(F32)
        n = x * lax.rsqrt(jnp.mean(x * x, axis=-1, keepdims=True) + 1e-06) * g
        out[:, at] = (n * c + pltpu.roll(n, 64, 1) * s).astype(BF16)


def finish(own, r1, r2, gain, cosine, sine, rows=768):
    t, width = own.shape
    wide = pl.BlockSpec((rows, width), lambda i: (i, 0))
    narrow = pl.BlockSpec((rows, 128), lambda i: (i, 0))
    return call(
        finish_kernel,
        jax.ShapeDtypeStruct((t, width), BF16),
        flops=20 * t * width,
        nbytes=14 * t * width,
        grid=(t // rows,),
        in_specs=[wide, pl.BlockSpec((rows, width), lambda i: (i, 1)), wide]
        + [pl.BlockSpec((1, 128), lambda i: (0, 0)), narrow, narrow],
        out_specs=wide,
    )(own, r1, r2, gain.reshape(1, 128), cosine, sine)


def tables(span_begin, t):
    lane = jnp.arange(128, dtype=jnp.int32)
    frequency = jnp.exp((lane % 64).astype(F32) * (-2.0 * math.log(1000000.0) / 128))
    k = jnp.arange(t // 32 + 32, dtype=jnp.int32)
    steps = jnp.where(k < t // 32, span_begin + 32 * k, k - t // 32)
    angles = steps.astype(F32)[:, None] * frequency[None, :]
    sign = jnp.where(lane < 64, -1.0, 1.0).astype(F32)
    c, s = lax.optimization_barrier((jnp.cos(angles), jnp.sin(angles)))
    ca, sa = c[: t // 32, None, :], s[: t // 32, None, :]
    cb, sb = c[None, t // 32 :, :], s[None, t // 32 :, :]
    cosine = ca * cb - sa * sb
    sine = (sa * cb + ca * sb) * sign
    return cosine.reshape(t, 128), sine.reshape(t, 128)


def spread_kernel(w, out):
    x = w[...].astype(F32)
    rows = jnp.concatenate([x[:, 0, :], x[:, 1, :]], axis=0).astype(BF16)
    for k in range(4):
        for t in range(4):
            out[k * 4 + t] = rows[:, t * 256 : (t + 1) * 256]


def fold(x):
    wide = jnp.concatenate([x[:40], x[40:]], axis=1)
    return jnp.concatenate([wide, jnp.zeros((8, 256), F32)], axis=0)


def unfold(x):
    return jnp.concatenate([x[:40, :128], x[:40, 128:]], axis=0)


def merge_kernel(x, outa, outb):
    mine = lax.axis_index("yl") * 8
    for xh in range(2):
        lines = [x[mine + xh * 4 + t].astype(F32) for t in range(4)]
        one, two = (
            jnp.concatenate([line[k * 20 : k * 20 + 20] for line in lines], axis=0)
            for k in range(2)
        )
        outa[xh * 80 : xh * 80 + 80, :] = one.astype(BF16)
        if xh == 1:
            outa[160:208, :] = fold(two[:, 128:]).astype(BF16)
    for yl in range(2):
        for xh in range(2):
            lines = [x[yl * 8 + xh * 4 + t].astype(F32) for t in range(4)]
            two = jnp.concatenate([line[20:40] for line in lines], axis=0)
            if xh == 0:
                outb[yl * 128 : yl * 128 + 80, :] = two.astype(BF16)
            else:
                outb[yl * 128 + 80 : yl * 128 + 128, :] = fold(two[:, :128]).astype(BF16)


def stack_kernel(own, other, out):
    yh = lax.axis_index("yh")
    for d, ref in enumerate((own, other)):
        for yl in range(2):
            at = lax.rem(yh + d, 2) * 2 + yl
            out[pl.ds(pl.multiple_of(at * 80, 16), 80), :] = ref[yl * 128 : yl * 128 + 80, :]
            col = pl.multiple_of(at // 2 * 128, 128)
            side = unfold(ref[yl * 128 + 80 : yl * 128 + 128, :].astype(F32))
            out[320 + yl * 80 : 400 + yl * 80, pl.ds(col, 128)] = side.astype(BF16)


def rows_kernel(*refs):
    z = lax.axis_index("z")
    out = refs[-1]
    for d in range(8):
        at = lax.rem(z + d, 8)
        for h in range(2):
            row = pl.multiple_of(320 + at * 80 + h * 640, 16)
            out[pl.ds(row, 80), :] = refs[d][h * 80 : h * 80 + 80, :]
        row = pl.multiple_of(lax.rem(at, 4) * 80, 16)
        col = pl.multiple_of(at // 4 * 128, 128)
        out[pl.ds(row, 80), pl.ds(col, 128)] = unfold(refs[d][160:208, :].astype(F32)).astype(BF16)


def small(kernel, shapes, *arrays):
    single = len(shapes) == 1
    out = [jax.ShapeDtypeStruct(s, BF16) for s in shapes]
    return call(
        kernel,
        out[0] if single else out,
        nbytes=4 * sum(math.prod(s) for s in shapes),
        in_specs=[VMEM] * len(arrays),
        out_specs=VMEM if single else [VMEM] * len(out),
    )(*arrays)


def scale_blocks(x, start, count, first, put, bm):
    lane = lax.broadcasted_iota(jnp.int32, (1, 128), 1)
    for j in range(2):
        row = bm[j : j + 1, :]
        for k in range(count // 128):
            blk = x[start + k * 128 : start + (k + 1) * 128, j * 128 : (j + 1) * 128]
            top = jnp.max(jnp.abs(blk), axis=0, keepdims=True).astype(F32)
            m = jnp.max(top, axis=1, keepdims=True) + 1e-06
            put(k, j, (blk.astype(F32) * (1.0 / m)).astype(BF16))
            row = jnp.where(lane == first + k, m, row)
        bm[j : j + 1, :] = row


def y_at(offsets, i):
    d = offsets[0]
    for u, other in enumerate(offsets[1:], 1):
        d = jnp.where(i == u, other, d)
    return lax.rem(lax.axis_index(Y) + d, 4)


def scale_groups_kernel(groups, offsets, n, *refs):
    ins, out, bm = refs[:n], refs[-2], refs[-1]
    i = pl.program_id(0)
    y = lax.axis_index(Y)

    @pl.when(i == 0)
    def _():
        bm[...] = refs[n][...] if len(refs) > n + 2 else jnp.zeros_like(bm)

    for u, group in enumerate(groups):

        @pl.when(i == u)
        def _(u=u, group=group):
            row = 0
            for k, start, count in group:
                base = row

                def put(r, j, v):
                    out[0, base + r * 128 : base + (r + 1) * 128, j * 128 : (j + 1) * 128] = v

                first = lax.rem(y + offsets[u], 4) * 10 + row // 128
                scale_blocks(ins[k], start, count, first, put, bm)
                row += count


def scale_groups(pieces, groups, offsets, done=None):
    n = len(pieces)
    ins = list(pieces)
    alias = {}
    if done is not None:
        ins += [done[1], done[0]]
        alias = {n + 1: 0, n: 1}
    in_specs = [pl.BlockSpec(p.shape, lambda i: (0, 0)) for p in ins[: n + 1]]
    if done is not None:
        in_specs.append(pl.BlockSpec(memory_space=pl.ANY))
    return call(
        functools.partial(scale_groups_kernel, groups, offsets, n),
        [jax.ShapeDtypeStruct((2, 5120, 256), BF16), jax.ShapeDtypeStruct((2, 128), F32)],
        flops=len(groups) * 1280 * 256 * 8,
        nbytes=len(groups) * 1280 * 256 * 4,
        grid=(len(groups),),
        in_specs=in_specs,
        out_specs=[
            pl.BlockSpec((1, 1280, 256), lambda i: (0, y_at(offsets, i), 0)),
            pl.BlockSpec((2, 128), lambda i: (0, 0)),
        ],
        input_output_aliases=alias,
    )(*ins)


def scale_last_kernel(*refs):
    z, y = lax.axis_index("z"), lax.axis_index(Y)
    whole, half, low, high, part, extra = refs[:7], refs[7:14], *refs[14:17], refs[17:20]
    far0, far1, bma, _, out, bm, held, acc, acc0 = refs[20:]
    i = pl.program_id(0)

    def put(r, j, v):
        out[0, r * 128 : (r + 1) * 128, j * 128 : (j + 1) * 128] = v

    def row(d):
        return pl.multiple_of(lax.rem(z + d, 8) * 80, 16)

    def place(d, ref):
        held[pl.ds(row(d), 80), :] = ref[...]

    @pl.when(i == 0)
    def _():
        acc[...] = jnp.zeros_like(acc)
        acc0[...] = bma[...]

    @pl.when(i < 4)
    def _():
        col = pl.multiple_of(i // 2 * 128, 128)
        for d, ref, side in zip((0, 1, 2, 3, 5, 6, 7), whole, half):
            place(d, ref)
            held[pl.ds(row(d) + 640, 80), 0:128] = side[:, pl.ds(col, 128)]
        held[pl.ds(row(4) + 640, 80), 0:128] = part[:, pl.ds(col, 128)]

    @pl.when(i < 3)
    def _():
        place(4, low)

    @pl.when(i == 3)
    def _():
        place(4, high)

    for d, ref in zip((0, 1, 2, 3), (extra[0], extra[1], far0, extra[2])):

        @pl.when((lax.rem(y + d, 4) == i) & (i < 4))
        def _(ref=ref):
            held[640:960, 128:256] = ref[0:320, 0:128]
            held[960:1280, 128:256] = ref[0:320, 128:256]

    @pl.when(i < 4)
    def _():
        scale_blocks(held, 0, 1280, i * 10, put, acc)

    @pl.when(i == 4)
    def _():
        held[0:480, :] = far0[320:800, :]
        held[480:1280, :] = far1[...]
        scale_blocks(held, 0, 1280, lax.rem(y + 2, 4) * 10, put, acc0)
        bm[0] = acc0[:, :40]
        bm[1] = acc[:, :40]


def scale_last(pieces, low, high, extra, far0, far1, done):
    part = (80, 256)
    at = lambda i: jnp.minimum(i, 3)
    return call(
        scale_last_kernel,
        [jax.ShapeDtypeStruct((2, 5120, 256), BF16), jax.ShapeDtypeStruct((2, 2, 40), F32)],
        flops=6400 * 256 * 8,
        nbytes=6400 * 256 * 4,
        grid=(5,),
        in_specs=[pl.BlockSpec(part, lambda i: (at(i), 0))] * 7
        + [pl.BlockSpec(part, lambda i: (4 + lax.rem(at(i), 2), 0))] * 7
        + [
            pl.BlockSpec(part, lambda i: (jnp.minimum(i, 2), 0)),
            pl.BlockSpec(part, lambda i: (0, 0)),
            pl.BlockSpec(part, lambda i: (1 + lax.rem(at(i), 2), 0)),
        ]
        + [pl.BlockSpec((320, 256), lambda i: (0, 0))] * 3
        + [pl.BlockSpec((800, 256), lambda i: (0, 0))] * 2
        + [
            pl.BlockSpec((2, 128), lambda i: (0, 0)),
            pl.BlockSpec(memory_space=pl.ANY),
        ],
        out_specs=[
            pl.BlockSpec(
                (1, 1280, 256),
                lambda i: (
                    jnp.where(i < 4, 1, 0),
                    jnp.where(i < 4, i, lax.rem(lax.axis_index(Y) + 2, 4)),
                    0,
                ),
            ),
            pl.BlockSpec((2, 2, 40), lambda i: (0, 0, 0)),
        ],
        scratch_shapes=[
            pltpu.VMEM((1280, 256), BF16),
            pltpu.VMEM((2, 128), F32),
            pltpu.VMEM((2, 128), F32),
        ],
        input_output_aliases={23: 0},
    )(*pieces, *pieces, low, high, high, *extra, far0, far1, done[1], done[0])


def body(activations, key_weight, key_gain, span_start, next_weight):
    line = small(spread_kernel, [(16, 40, 256)], next_weight.transpose(1, 0, 2))
    line = lax.all_to_all(line, ("yl", "xh", "xl", "c"), split_axis=0, concat_axis=0, tiled=True)
    pair, mid, own = project(activations, key_weight)
    line, pair = after((line, pair))
    a0, b0 = small(merge_kernel, [(208, 256), (256, 256)], line)

    az = {0: a0}
    az[1], az[7] = shift(a0, "z", -1), shift(a0, "z", 1)
    other = shift(b0, "yh", 1)
    az[2], az[6] = shift(az[1], "z", -1), shift(az[7], "z", 1)
    az[3], az[5] = shift(az[2], "z", -1), shift(az[6], "z", 1)
    az[4] = shift(az[3], "z", -1)
    mb = small(stack_kernel, [(480, 256)], b0, other)
    ma = small(rows_kernel, [(1600, 256)], *[az[d] for d in range(8)])
    mb, ma, pair = after((mb, ma, pair))

    bz = {0: mb}
    bz[1], bz[7] = shift(mb, "z", -1), shift(mb, "z", 1)
    up, down = shift(ma, Y, -1), shift(ma, Y, 1)
    r1 = shift(pair, "c", 1)
    half = add(mid, r1)
    bz[1], bz[7], half = after((bz[1], bz[7], half))
    r2 = shift(half, "xl", 1)
    bz[2], bz[6] = shift(bz[1], "z", -1), shift(bz[7], "z", 1)
    done = scale_groups([ma], [[(0, 320, 1280)]], [0])
    bz[2], bz[6], *done = after((bz[2], bz[6], *done))
    bz[3], bz[5] = shift(bz[2], "z", -1), shift(bz[6], "z", 1)
    far0 = shift(up[:800], Y, -1)
    far1 = shift(down[800:], Y, 1)
    done = scale_groups([up, down], [[(0, 320, 1280)], [(1, 320, 1280)]], [1, 3], done)
    bz[3], bz[5], *done = after((bz[3], bz[5], *done))
    low = shift(bz[3][:240], "z", -1)
    high = shift(bz[5][240:], "z", 1)
    cosine, sine = tables(span_start[0], activations.shape[0])
    new_keys = finish(own, r1, r2, key_gain, cosine, sine)
    low, high, far0, far1, new_keys, *done = after((low, high, far0, far1, new_keys, *done))
    pieces = [bz[d] for d in (0, 1, 2, 3, 5, 6, 7)]
    next_scaled, block_max = scale_last(pieces, low, high, [ma, up, down], far0, far1, done)
    return new_keys, next_scaled, block_max.transpose(0, 2, 1)


def solution(mesh):
    line = Mesh(mesh.devices.reshape(SIZES), AXES)
    fsdp, tensor = (*Y, "xh", "z"), ("xl", "c")
    placed = (
        P(fsdp, tensor),
        P(tensor, None),
        P(),
        P(fsdp),
        P(None, fsdp + tensor, None),
    )
    return jax.shard_map(
        body,
        mesh=line,
        in_specs=placed,
        out_specs=(P(fsdp, tensor), P(None, None, tensor), P(None, None, tensor)),
        check_vma=False,
    )
```

```python
import functools
import math

import jax
import jax.numpy as jnp
from jax import lax
from jax.experimental import pallas as pl
from jax.experimental.pallas import tpu as pltpu
from jax.sharding import Mesh
from jax.sharding import PartitionSpec as P

BLOCK = 128
AXES = ("yh", "yl", "xh", "z", "xl", "c")
SIZES = (2, 2, 2, 8, 2, 2)
Y = ("yh", "yl")
F32 = jnp.float32
BF16 = jnp.bfloat16
MIB = 1024 * 1024
NA = 3


after = lax.optimization_barrier


def shift(x, axis, step):
    n = 4 if axis == Y else SIZES[AXES.index(axis)]
    return lax.ppermute(x, axis, [(i, (i + step) % n) for i in range(n)])


def call(kernel, out_shape, flops=0, nbytes=0, vmem=16, **kw):
    return pl.pallas_call(
        kernel,
        out_shape=out_shape,
        compiler_params=pltpu.CompilerParams(vmem_limit_bytes=vmem * MIB),
        cost_estimate=pl.CostEstimate(flops=flops, bytes_accessed=nbytes, transcendentals=0),
        **kw,
    )


VMEM = pl.BlockSpec(memory_space=pltpu.VMEM)


def project_kernel(a, w, pair, mid, own, av, wv, asem, wsem):
    n, rows = av.shape[0], av.shape[1]
    xl, c = lax.axis_index("xl"), lax.axis_index("c")
    tiles = [3 - 2 * xl - c, 2 * xl + 1 - c, 2 - 2 * xl + c, 2 * xl + c]

    def get_w(k):
        at = pl.multiple_of(tiles[k] * 256, 256)
        return pltpu.make_async_copy(w.at[:, pl.ds(at, 256)], wv.at[k], wsem.at[k])

    def get_a(i):
        return pltpu.make_async_copy(a.at[pl.ds(i * rows, rows), :], av.at[i], asem.at[i])

    get_a(0).start()
    for k in range(4):
        get_w(k).start()
    for i in range(1, n):
        get_a(i).start()
    for i in range(n):
        get_a(i).wait()
        at = slice(i * rows, (i + 1) * rows)
        for k, (out, col) in enumerate([(pair, 0), (pair, 256), (mid, 0), (own, 0)]):
            if i == 0:
                get_w(k).wait()
            p = jnp.dot(av[i], wv[k], preferred_element_type=F32)
            out[at, col : col + 256] = p.astype(BF16)


def project(a, w, n=NA):
    t, d = a.shape
    width = w.shape[1] // 4
    hbm = pl.BlockSpec(memory_space=pltpu.HBM)
    return call(
        project_kernel,
        [jax.ShapeDtypeStruct((t, k * width), BF16) for k in (2, 1, 1)],
        flops=8 * t * d * width,
        nbytes=2 * t * d + 8 * d * width + 8 * t * width,
        vmem=58,
        in_specs=[hbm, hbm],
        out_specs=[VMEM] * 3,
        scratch_shapes=[
            pltpu.VMEM((n, t // n, d), BF16),
            pltpu.VMEM((4, d, width), BF16),
            pltpu.SemaphoreType.DMA((n,)),
            pltpu.SemaphoreType.DMA((4,)),
        ],
    )(a, w)


def add_kernel(x, r, out):
    out[...] = (x[...].astype(F32) + r[...].astype(F32)).astype(BF16)


def add(x, r, rows=768):
    t, width = x.shape
    spec = pl.BlockSpec((rows, width), lambda i: (i, 0))
    return call(
        add_kernel,
        jax.ShapeDtypeStruct((t, width), BF16),
        flops=t * width,
        nbytes=6 * t * width,
        grid=(t // rows,),
        in_specs=[spec, pl.BlockSpec((rows, width), lambda i: (i, 0))],
        out_specs=spec,
    )(x, r)


def finish_kernel(own, r1, r2, gain, cosine, sine, out):
    g = gain[...]
    c = cosine[...]
    s = sine[...]
    for h in range(2):
        at = slice(h * 128, (h + 1) * 128)
        x = own[:, at].astype(F32) + r1[:, at].astype(F32) + r2[:, at].astype(F32)
        n = x * lax.rsqrt(jnp.mean(x * x, axis=-1, keepdims=True) + 1e-06) * g
        out[:, at] = (n * c + pltpu.roll(n, 64, 1) * s).astype(BF16)


def finish(own, r1, r2, gain, cosine, sine, rows=768):
    t, width = own.shape
    wide = pl.BlockSpec((rows, width), lambda i: (i, 0))
    narrow = pl.BlockSpec((rows, 128), lambda i: (i, 0))
    return call(
        finish_kernel,
        jax.ShapeDtypeStruct((t, width), BF16),
        flops=20 * t * width,
        nbytes=14 * t * width,
        grid=(t // rows,),
        in_specs=[wide, pl.BlockSpec((rows, width), lambda i: (i, 1)), wide]
        + [pl.BlockSpec((1, 128), lambda i: (0, 0)), narrow, narrow],
        out_specs=wide,
    )(own, r1, r2, gain.reshape(1, 128), cosine, sine)


def tables(span_begin, t):
    lane = jnp.arange(128, dtype=jnp.int32)
    frequency = jnp.exp((lane % 64).astype(F32) * (-2.0 * math.log(1000000.0) / 128))
    k = jnp.arange(t // 32 + 32, dtype=jnp.int32)
    steps = jnp.where(k < t // 32, span_begin + 32 * k, k - t // 32)
    angles = steps.astype(F32)[:, None] * frequency[None, :]
    sign = jnp.where(lane < 64, -1.0, 1.0).astype(F32)
    c, s = lax.optimization_barrier((jnp.cos(angles), jnp.sin(angles)))
    ca, sa = c[: t // 32, None, :], s[: t // 32, None, :]
    cb, sb = c[None, t // 32 :, :], s[None, t // 32 :, :]
    cosine = ca * cb - sa * sb
    sine = (sa * cb + ca * sb) * sign
    return cosine.reshape(t, 128), sine.reshape(t, 128)


def spread_kernel(w, out):
    x = w[...].astype(F32)
    rows = jnp.concatenate([x[:, 0, :], x[:, 1, :]], axis=0).astype(BF16)
    for k in range(4):
        for t in range(4):
            out[k * 4 + t] = rows[:, t * 256 : (t + 1) * 256]


def fold(x):
    wide = jnp.concatenate([x[:40], x[40:]], axis=1)
    return jnp.concatenate([wide, jnp.zeros((8, 256), F32)], axis=0)


def unfold(x):
    return jnp.concatenate([x[:40, :128], x[:40, 128:]], axis=0)


def merge_kernel(x, outa, outb):
    mine = lax.axis_index("yl") * 8
    for xh in range(2):
        lines = [x[mine + xh * 4 + t].astype(F32) for t in range(4)]
        one, two = (
            jnp.concatenate([line[k * 20 : k * 20 + 20] for line in lines], axis=0)
            for k in range(2)
        )
        outa[xh * 80 : xh * 80 + 80, :] = one.astype(BF16)
        if xh == 1:
            outa[160:208, :] = fold(two[:, 128:]).astype(BF16)
    for yl in range(2):
        for xh in range(2):
            lines = [x[yl * 8 + xh * 4 + t].astype(F32) for t in range(4)]
            two = jnp.concatenate([line[20:40] for line in lines], axis=0)
            if xh == 0:
                outb[yl * 128 : yl * 128 + 80, :] = two.astype(BF16)
            else:
                outb[yl * 128 + 80 : yl * 128 + 128, :] = fold(two[:, :128]).astype(BF16)


def stack_kernel(own, other, out):
    yh = lax.axis_index("yh")
    for d, ref in enumerate((own, other)):
        for yl in range(2):
            at = lax.rem(yh + d, 2) * 2 + yl
            out[pl.ds(pl.multiple_of(at * 80, 16), 80), :] = ref[yl * 128 : yl * 128 + 80, :]
            col = pl.multiple_of(at // 2 * 128, 128)
            side = unfold(ref[yl * 128 + 80 : yl * 128 + 128, :].astype(F32))
            out[320 + yl * 80 : 400 + yl * 80, pl.ds(col, 128)] = side.astype(BF16)


def rows_kernel(*refs):
    z = lax.axis_index("z")
    out = refs[-1]
    for d in range(8):
        at = lax.rem(z + d, 8)
        for h in range(2):
            row = pl.multiple_of(320 + at * 80 + h * 640, 16)
            out[pl.ds(row, 80), :] = refs[d][h * 80 : h * 80 + 80, :]
        row = pl.multiple_of(lax.rem(at, 4) * 80, 16)
        col = pl.multiple_of(at // 4 * 128, 128)
        out[pl.ds(row, 80), pl.ds(col, 128)] = unfold(refs[d][160:208, :].astype(F32)).astype(BF16)


def small(kernel, shapes, *arrays):
    single = len(shapes) == 1
    out = [jax.ShapeDtypeStruct(s, BF16) for s in shapes]
    return call(
        kernel,
        out[0] if single else out,
        nbytes=4 * sum(math.prod(s) for s in shapes),
        in_specs=[VMEM] * len(arrays),
        out_specs=VMEM if single else [VMEM] * len(out),
    )(*arrays)


def scale_blocks(x, start, count, first, put, bm):
    lane = lax.broadcasted_iota(jnp.int32, (1, 128), 1)
    for j in range(2):
        row = bm[j : j + 1, :]
        for k in range(count // 128):
            blk = x[start + k * 128 : start + (k + 1) * 128, j * 128 : (j + 1) * 128]
            top = jnp.max(jnp.abs(blk), axis=0, keepdims=True).astype(F32)
            m = jnp.max(top, axis=1, keepdims=True) + 1e-06
            put(k, j, (blk.astype(F32) * (1.0 / m)).astype(BF16))
            row = jnp.where(lane == first + k, m, row)
        bm[j : j + 1, :] = row


def y_at(offsets, i):
    d = offsets[0]
    for u, other in enumerate(offsets[1:], 1):
        d = jnp.where(i == u, other, d)
    return lax.rem(lax.axis_index(Y) + d, 4)


def scale_groups_kernel(groups, offsets, n, *refs):
    ins, out, bm = refs[:n], refs[-2], refs[-1]
    i = pl.program_id(0)
    y = lax.axis_index(Y)

    @pl.when(i == 0)
    def _():
        bm[...] = refs[n][...] if len(refs) > n + 2 else jnp.zeros_like(bm)

    for u, group in enumerate(groups):

        @pl.when(i == u)
        def _(u=u, group=group):
            row = 0
            for k, start, count in group:
                base = row

                def put(r, j, v):
                    out[0, base + r * 128 : base + (r + 1) * 128, j * 128 : (j + 1) * 128] = v

                first = lax.rem(y + offsets[u], 4) * 10 + row // 128
                scale_blocks(ins[k], start, count, first, put, bm)
                row += count


def scale_groups(pieces, groups, offsets, done=None):
    n = len(pieces)
    ins = list(pieces)
    alias = {}
    if done is not None:
        ins += [done[1], done[0]]
        alias = {n + 1: 0, n: 1}
    in_specs = [pl.BlockSpec(p.shape, lambda i: (0, 0)) for p in ins[: n + 1]]
    if done is not None:
        in_specs.append(pl.BlockSpec(memory_space=pl.ANY))
    return call(
        functools.partial(scale_groups_kernel, groups, offsets, n),
        [jax.ShapeDtypeStruct((2, 5120, 256), BF16), jax.ShapeDtypeStruct((2, 128), F32)],
        flops=len(groups) * 1280 * 256 * 8,
        nbytes=len(groups) * 1280 * 256 * 4,
        grid=(len(groups),),
        in_specs=in_specs,
        out_specs=[
            pl.BlockSpec((1, 1280, 256), lambda i: (0, y_at(offsets, i), 0)),
            pl.BlockSpec((2, 128), lambda i: (0, 0)),
        ],
        input_output_aliases=alias,
    )(*ins)


def near_y(i):
    return lax.rem(lax.axis_index(Y) + jnp.where(i == 2, 3, i), 4)


def far_y(i):
    return lax.rem(lax.axis_index(Y) + 2, 4)


def put_in(out):
    def put(r, j, v):
        out[0, r * 128 : (r + 1) * 128, j * 128 : (j + 1) * 128] = v

    return put


def gather_rows(i, refs, held):
    z = lax.axis_index("z")
    whole, half, low, high, part = refs[:7], refs[7:14], *refs[14:17]
    col = pl.multiple_of(i // 2 * 128, 128)

    def row(d):
        return pl.multiple_of(lax.rem(z + d, 8) * 80, 16)

    for d, ref, side in zip((0, 1, 2, 3, 5, 6, 7), whole, half):
        held[pl.ds(row(d), 80), :] = ref[...]
        held[pl.ds(row(d) + 640, 80), 0:128] = side[:, pl.ds(col, 128)]
    held[pl.ds(row(4) + 640, 80), 0:128] = part[:, pl.ds(col, 128)]

    @pl.when(i < 3)
    def _():
        held[pl.ds(row(4), 80), :] = low[...]

    @pl.when(i == 3)
    def _():
        held[pl.ds(row(4), 80), :] = high[...]


def side_rows(ref, held):
    held[640:960, 128:256] = ref[0:320, 0:128]
    held[960:1280, 128:256] = ref[0:320, 128:256]


def scale_near_kernel(*refs):
    extra = refs[17:20]
    _, out, acc, held = refs[20:]
    step = pl.program_id(0)
    i = near_y(step)

    @pl.when(step == 0)
    def _():
        acc[...] = jnp.zeros_like(acc)

    gather_rows(i, refs, held)
    for k in range(3):

        @pl.when(step == k)
        def _(k=k):
            side_rows(extra[k], held)

    scale_blocks(held, 0, 1280, i * 10, put_in(out), acc)


def scale_far_kernel(*refs):
    far0, far1, bma, near, _, out, bm, held, acc, acc0 = refs[17:]
    step = pl.program_id(0)
    i = far_y(step)

    @pl.when(step == 0)
    def _():
        acc[...] = near[...]
        gather_rows(i, refs, held)
        side_rows(far0, held)
        scale_blocks(held, 0, 1280, i * 10, put_in(out), acc)

    @pl.when(step == 1)
    def _():
        acc0[...] = bma[...]
        held[0:480, :] = far0[320:800, :]
        held[480:1280, :] = far1[...]
        scale_blocks(held, 0, 1280, i * 10, put_in(out), acc0)
        bm[0] = acc0[:, :40]
        bm[1] = acc[:, :40]


def ring_specs(at):
    part = (80, 256)
    return (
        [pl.BlockSpec(part, lambda i: (at(i), 0))] * 7
        + [pl.BlockSpec(part, lambda i: (4 + lax.rem(at(i), 2), 0))] * 7
        + [
            pl.BlockSpec(part, lambda i: (jnp.minimum(at(i), 2), 0)),
            pl.BlockSpec(part, lambda i: (0, 0)),
            pl.BlockSpec(part, lambda i: (1 + lax.rem(at(i), 2), 0)),
        ]
    )


def scale_near(ring, extra, buffer):
    return call(
        scale_near_kernel,
        [jax.ShapeDtypeStruct((2, 5120, 256), BF16), jax.ShapeDtypeStruct((2, 128), F32)],
        flops=3840 * 256 * 8,
        nbytes=3840 * 256 * 4,
        grid=(3,),
        in_specs=ring_specs(near_y)
        + [pl.BlockSpec((320, 256), lambda i: (0, 0))] * 3
        + [pl.BlockSpec(memory_space=pl.ANY)],
        out_specs=[
            pl.BlockSpec((1, 1280, 256), lambda i: (1, near_y(i), 0)),
            pl.BlockSpec((2, 128), lambda i: (0, 0)),
        ],
        scratch_shapes=[pltpu.VMEM((1280, 256), BF16)],
        input_output_aliases={20: 0},
    )(*ring, *extra, buffer)


def scale_far(ring, far0, far1, bma, near, buffer):
    return call(
        scale_far_kernel,
        [jax.ShapeDtypeStruct((2, 5120, 256), BF16), jax.ShapeDtypeStruct((2, 2, 40), F32)],
        flops=2560 * 256 * 8,
        nbytes=2560 * 256 * 4,
        grid=(2,),
        in_specs=ring_specs(far_y)
        + [pl.BlockSpec((800, 256), lambda i: (0, 0))] * 2
        + [pl.BlockSpec((2, 128), lambda i: (0, 0))] * 2
        + [pl.BlockSpec(memory_space=pl.ANY)],
        out_specs=[
            pl.BlockSpec((1, 1280, 256), lambda i: (1 - i, far_y(i), 0)),
            pl.BlockSpec((2, 2, 40), lambda i: (0, 0, 0)),
        ],
        scratch_shapes=[
            pltpu.VMEM((1280, 256), BF16),
            pltpu.VMEM((2, 128), F32),
            pltpu.VMEM((2, 128), F32),
        ],
        input_output_aliases={21: 0},
    )(*ring, far0, far1, bma, near, buffer)


def body(activations, key_weight, key_gain, span_start, next_weight):
    line = small(spread_kernel, [(16, 40, 256)], next_weight.transpose(1, 0, 2))
    line = lax.all_to_all(line, ("yl", "xh", "xl", "c"), split_axis=0, concat_axis=0, tiled=True)
    pair, mid, own = project(activations, key_weight)
    line, pair = after((line, pair))
    a0, b0 = small(merge_kernel, [(208, 256), (256, 256)], line)

    az = {0: a0}
    az[1], az[7] = shift(a0, "z", -1), shift(a0, "z", 1)
    other = shift(b0, "yh", 1)
    az[2], az[6] = shift(az[1], "z", -1), shift(az[7], "z", 1)
    az[3], az[5] = shift(az[2], "z", -1), shift(az[6], "z", 1)
    az[4] = shift(az[3], "z", -1)
    mb = small(stack_kernel, [(480, 256)], b0, other)
    ma = small(rows_kernel, [(1600, 256)], *[az[d] for d in range(8)])
    mb, ma, pair = after((mb, ma, pair))

    bz = {0: mb}
    bz[1], bz[7] = shift(mb, "z", -1), shift(mb, "z", 1)
    up, down = shift(ma, Y, -1), shift(ma, Y, 1)
    r1 = shift(pair, "c", 1)
    half = add(mid, r1)
    bz[1], bz[7], half = after((bz[1], bz[7], half))
    r2 = shift(half, "xl", 1)
    bz[2], bz[6] = shift(bz[1], "z", -1), shift(bz[7], "z", 1)
    done = scale_groups([ma], [[(0, 320, 1280)]], [0])
    bz[2], bz[6], *done = after((bz[2], bz[6], *done))
    bz[3], bz[5] = shift(bz[2], "z", -1), shift(bz[6], "z", 1)
    far0 = shift(up[:800], Y, -1)
    far1 = shift(down[800:], Y, 1)
    done = scale_groups([up, down], [[(0, 320, 1280)], [(1, 320, 1280)]], [1, 3], done)
    bz[3], bz[5], *done = after((bz[3], bz[5], *done))
    low = shift(bz[3][:240], "z", -1)
    high = shift(bz[5][240:], "z", 1)
    cosine, sine = tables(span_start[0], activations.shape[0])
    new_keys = finish(own, r1, r2, key_gain, cosine, sine)
    low, high, new_keys, *done = after((low, high, new_keys, *done))
    pieces = [bz[d] for d in (0, 1, 2, 3, 5, 6, 7)]
    ring = [*pieces, *pieces, low, high, high]
    buffer, near = scale_near(ring, [ma, up, down], done[0])
    far0, far1, buffer, near = after((far0, far1, buffer, near))
    next_scaled, block_max = scale_far(ring, far0, far1, done[1], near, buffer)
    return new_keys, next_scaled, block_max.transpose(0, 2, 1)


def solution(mesh):
    line = Mesh(mesh.devices.reshape(SIZES), AXES)
    fsdp, tensor = (*Y, "xh", "z"), ("xl", "c")
    placed = (
        P(fsdp, tensor),
        P(tensor, None),
        P(),
        P(fsdp),
        P(None, fsdp + tensor, None),
    )
    return jax.shard_map(
        body,
        mesh=line,
        in_specs=placed,
        out_specs=(P(fsdp, tensor), P(None, None, tensor), P(None, None, tensor)),
        check_vma=False,
    )
```
